32 devices in a mesh: section: 4 (over x, core), seq: 8 (over z, y).
Axes of the slice: x: 2, y: 2, z: 4, core: 2. Of those that a mesh axis runs over, the one named last changes fastest.
Arguments:
- q_img: bfloat16 [1024, 3072], P('seq', 'section'), may hold values from -6 to 6
- k_img: bfloat16 [1024, 3072], P('seq', 'section'), may hold values from -6 to 6
- v_img: bfloat16 [1024, 3072], P('seq', 'section'), may hold values from -6 to 6
- q_txt: bfloat16 [256, 3072], P('seq', 'section'), may hold values from -6 to 6
- k_txt: bfloat16 [256, 3072], P('seq', 'section'), may hold values from -6 to 6
- v_txt: bfloat16 [256, 3072], P('seq', 'section'), may hold values from -6 to 6
- norm_gains: float32 [4, 128], replicated, may hold values from 1.2 to 2
- block_map: int32 [24, 8, 8], P('section', 'seq'), may hold values 0 or 1
Outputs:
- image_out: bfloat16 [256, 4, 3072], P('seq', 'section')
- text_out: bfloat16 [256, 3072], P('seq', 'section')
The draws below stay inside these ranges and needn't reach their ends.
All inputs are finite; a program needn't handle non-finite values. No bound on the sum of `block_map` on one device may be relied on, other than what follows from the above.
Results may differ from the reference program's by a relative error of at most 0.011.
Values may be sent and summed in bfloat16 or wider, within the bound.
A program may use at most 256 MiB of HBM per device.

```python
import math
import jax
import jax.numpy as jnp
from jax import lax

HEADS = 24
DH = 128
BLOCK = 128
TXT = 256
IMG = 1024
NB = 8
N_SECTION = 4


def with_ends(entries, stream_key, low, largest):
    extent = entries.shape
    spot = [jax.random.randint(jax.random.fold_in(stream_key, axis), (), 0, extent[axis]) for axis in range(len(extent))]
    entries = entries.at[tuple(spot)].set(low)
    longest = extent.index(max(extent))
    spot[longest] = (spot[longest] + 1) % extent[longest]
    return entries.at[tuple(spot)].set(largest)


def level_of(own_key, extent, cuts, least, largest):
    def one(dim, parts):
        steps = jax.random.uniform(jax.random.fold_in(jax.random.fold_in(own_key, 6), dim), (parts,), jnp.float32, least / len(cuts), largest / len(cuts))
        return jnp.repeat(jnp.exp(steps), extent[dim] // parts).reshape((-1,) + (1,) * (len(extent) - dim - 1))

    level = one(*cuts[0])
    for cut in cuts[1:]:
        level = level * one(*cut)
    return level


def normal_values(own_key, shape, spread, most, cuts=(), kind=jnp.bfloat16):
    drawn = jax.random.normal(own_key, shape, jnp.float32) * spread
    if len(cuts) > 0:
        drawn = level_of(own_key, shape, cuts, -0.22, 0.18) * drawn
    return jnp.clip(drawn, min=-most, max=most).astype(kind)


def setup_inputs(seed: int = 0) -> dict:
    seeds = jax.random.split(jax.random.key(seed), 9)
    q_img = normal_values(seeds[0], (IMG, HEADS * DH), 1.0, 6.0, ((0, 8), (1, 4)))
    k_img = normal_values(seeds[1], (IMG, HEADS * DH), 1.0, 6.0, ((0, 8), (1, 4)))
    v_img = normal_values(seeds[2], (IMG, HEADS * DH), 1.0, 6.0, ((0, 8), (1, 4)))
    q_txt = normal_values(seeds[3], (TXT, HEADS * DH), 1.0, 6.0, ((0, 8), (1, 4)))
    k_txt = normal_values(seeds[4], (TXT, HEADS * DH), 1.0, 6.0, ((0, 8), (1, 4)))
    v_txt = normal_values(seeds[5], (TXT, HEADS * DH), 1.0, 6.0, ((0, 8), (1, 4)))
    norm_gains = jnp.clip(jnp.exp(jax.random.uniform(seeds[6], (4, DH), jnp.float32, math.log(1.2), math.log(2.0))), 1.2, 2.0)
    block_map = with_ends((jax.random.randint(seeds[7], (HEADS, NB, NB), 0, 2) < 1).astype(jnp.int32), jax.random.fold_in(seeds[7], 1), 0, 1)
    return dict(q_img=q_img, k_img=k_img, v_img=v_img, q_txt=q_txt, k_txt=k_txt, v_txt=v_txt, norm_gains=norm_gains, block_map=block_map)


def normed(values, gain):
    rows = values.shape[0]
    floats = values.astype(jnp.float32).reshape(rows, HEADS, DH)
    power = lax.optimization_barrier(jnp.mean(floats * floats, axis=-1, keepdims=True))
    return (floats * lax.rsqrt(power + 1e-06) * gain).astype(jnp.bfloat16)

def reference(q_img, k_img, v_img, q_txt, k_txt, v_txt, norm_gains, block_map):
    queries = jnp.concatenate([normed(q_img, norm_gains[0]), normed(q_txt, norm_gains[2])], axis=0)
    keys_all = jnp.concatenate([normed(k_img, norm_gains[1]), normed(k_txt, norm_gains[3])], axis=0)
    total = IMG + TXT
    values_all = jnp.concatenate([v_img, v_txt], axis=0).reshape(total, HEADS, DH)

    def per_head(pieces):
        query_head, key_head, value_head, flags = pieces
        scores = jnp.dot(query_head, key_head.T, preferred_element_type=jnp.float32) * DH ** (-0.5)
        image_mask = jnp.broadcast_to(flags[:, None, :, None] > 0, (NB, BLOCK, NB, BLOCK)).reshape(IMG, IMG)
        keep = jnp.pad(image_mask, ((0, TXT), (0, TXT)), constant_values=True)
        weights = jnp.where(keep, jnp.exp(scores), jnp.float32(0.0))
        denominator = lax.optimization_barrier(jnp.sum(weights, axis=-1))
        numerator = jnp.dot(weights.astype(jnp.bfloat16), value_head, preferred_element_type=jnp.float32)
        return numerator / denominator[:, None]
    result = lax.map(per_head, (queries.transpose(1, 0, 2), keys_all.transpose(1, 0, 2), values_all.transpose(1, 0, 2), block_map))
    merged = result.transpose(1, 0, 2).reshape(total, HEADS * DH).astype(jnp.bfloat16)
    image_out = merged[:IMG].reshape(IMG // N_SECTION, N_SECTION, HEADS * DH)
    text_out = merged[IMG:]
    return (image_out, text_out)
```

```python
import functools
import math

import jax
import jax.numpy as jnp
from jax import lax
from jax.experimental import pallas as pl
from jax.experimental.pallas import tpu as pltpu
from jax.sharding import PartitionSpec as P

BLOCK = 128


def normed(values, gain, heads):
    rows = values.shape[0]
    floats = values.astype(jnp.float32).reshape(rows, heads, gain.shape[0])
    power = jnp.mean(floats * floats, axis=-1, keepdims=True)
    return (floats * lax.rsqrt(power + 1e-06) * gain).astype(jnp.bfloat16)


def make_keep(flags, query_shards, shards, first, rows, text_rows):
    heads = flags.shape[0]
    key_blocks = rows // BLOCK
    stride = rows + text_rows
    picked = lax.dynamic_slice_in_dim(flags, first * key_blocks, shards * key_blocks, 2)
    picked = picked.reshape(heads, query_shards, key_blocks, shards, key_blocks)
    image_mask = jnp.broadcast_to(
        picked[:, :, :, None, :, :, None] > 0,
        (heads, query_shards, key_blocks, BLOCK, shards, key_blocks, BLOCK),
    )
    image_mask = image_mask.reshape(heads, query_shards, rows, shards, rows)
    keep = jnp.pad(
        image_mask, ((0, 0), (0, 0), (0, text_rows), (0, 0), (0, text_rows)), constant_values=True
    )
    return keep.reshape(heads, query_shards * stride, shards, stride)


def accumulate(queries, flags, query_shards, rows, text_rows, carry, pieces, start):
    numer, denom = carry
    piece_keys, piece_values = pieces
    heads = queries.shape[1]
    head_size = queries.shape[2]
    stride = rows + text_rows
    shards = piece_keys.shape[0] // stride
    first = start // stride
    keys_four = piece_keys.reshape(shards, stride, heads, head_size)
    values_four = piece_values.reshape(shards, stride, heads, head_size)
    scores = jnp.einsum(
        "qhd,skhd->hqsk", queries, keys_four, preferred_element_type=jnp.float32
    ) * head_size ** (-0.5)
    keep = make_keep(flags, query_shards, shards, first, rows, text_rows)
    weights = jnp.where(keep, jnp.exp(scores), jnp.float32(0.0))
    denom = denom + jnp.sum(weights, axis=(2, 3))
    numer = numer + jnp.einsum(
        "hqsk,skhd->hqd",
        weights.astype(jnp.bfloat16),
        values_four,
        preferred_element_type=jnp.float32,
    )
    return (numer, denom)


def body(q_img, k_img, v_img, q_txt, k_txt, v_txt, norm_gains, block_map):
    rows, width = q_img.shape
    head_size = norm_gains.shape[1]
    heads = width // head_size
    text_rows = q_txt.shape[0]
    stride = rows + text_rows
    queries = jnp.concatenate(
        [normed(q_img, norm_gains[0], heads), normed(q_txt, norm_gains[2], heads)], axis=0
    )
    keys_image = normed(k_img, norm_gains[1], heads).reshape(rows, width)
    keys_text = normed(k_txt, norm_gains[3], heads).reshape(text_rows, width)
    local_keys = jnp.concatenate([keys_image, keys_text], axis=0)
    local_values = jnp.concatenate([v_img, v_txt], axis=0)
    start_state = (
        jnp.zeros((heads, stride, head_size), jnp.float32),
        jnp.zeros((heads, stride), jnp.float32),
    )

    def fold_step(carry, pieces, start):
        return accumulate(queries, block_map, 1, rows, text_rows, carry, pieces, start)

    whole_keys, whole_values = (
        lax.all_gather(local_keys, "seq", axis=0, tiled=True),
        lax.all_gather(local_values, "seq", axis=0, tiled=True),
    )
    count_seq = lax.axis_size("seq")
    grouped = 1
    while (
        grouped * 2 <= count_seq
        and count_seq % (grouped * 2) == 0
        and (grouped * 2 * stride <= 1024)
    ):
        grouped = grouped * 2
    span = grouped * stride

    def step_over(index, carry):
        offset = index * span
        piece_keys = lax.dynamic_slice_in_dim(whole_keys, offset, span, 0)
        piece_values = lax.dynamic_slice_in_dim(whole_values, offset, span, 0)
        return fold_step(carry, (piece_keys, piece_values), offset)

    numer, denom = lax.fori_loop(0, count_seq // grouped, step_over, start_state)
    result = numer / denom[..., None]
    merged = result.transpose(1, 0, 2).reshape(stride, width).astype(jnp.bfloat16)
    image_part = merged[:rows]
    text_out = merged[rows:]
    sections = lax.axis_size("section")
    image_out = lax.all_to_all(
        image_part.reshape(rows // sections, sections, width),
        "section",
        split_axis=1,
        concat_axis=2,
        tiled=True,
    )
    return (image_out, text_out)


def owner_of(head, heads, odd):
    even_pick = head + lax.div(head + heads - 2, heads - 1) + lax.div(head, heads - 1)
    return odd * (head + 1) + (1 - odd) * even_pick


def head_of(place, heads, odd):
    last = heads + 1
    even_pick = place - lax.div(place + last - 1, last) - lax.div(place, last)
    return odd * (place - 1) + (1 - odd) * even_pick


def partner(place, step, count):
    total = 0
    bit = 1
    while bit < count:
        total = total + bit * lax.rem(lax.div(place, bit) + lax.div(step, bit), 2)
        bit *= 2
    return total


def head_kernel(
    heads, seqs, sections,
    q_img, k_img, v_img, q_txt, k_txt, v_txt, gains, flags_in,
    image_out, text_out,
    flags_own, flags_got, q_img_got, q_txt_got, k_img_got, k_txt_got, values, keys_t, total,
    image_stage, text_stage,
    send_sem, recv_sem, image_sent, text_sent, image_recv, text_recv,
):
    rows = q_img.shape[0]
    text_rows = q_txt.shape[0]
    size = gains.shape[1]
    key_blocks = flags_in.shape[2]
    part = rows // sections
    all_rows = seqs * rows
    factor = size ** (-0.5) * math.log2(math.e)
    section = lax.axis_index("section")
    me = lax.axis_index("seq")
    odd = lax.rem(section, 2)

    barrier = pltpu.get_barrier_semaphore()

    def greet(index, carry):
        to_section = lax.div(index, seqs)
        to_seq = lax.rem(index, seqs)

        @pl.when(jnp.logical_or(to_section != section, to_seq != me))
        def _():
            pl.semaphore_signal(
                barrier,
                inc=1,
                device_id={"section": to_section, "seq": to_seq},
                device_id_type=pl.DeviceIdType.MESH,
            )

        return carry

    lax.fori_loop(0, sections * seqs, greet, 0)
    for head in range(heads):
        for block in range(key_blocks):
            flags_own[head, block : block + 1, :] = jnp.full(
                (1, flags_own.shape[2]), flags_in[head, 0, block], jnp.int32
            )
    pl.semaphore_wait(barrier, sections * seqs - 1)

    def landing(kind, source):
        if kind == 0:
            return flags_got.at[source]
        if kind == 1:
            return k_img_got.at[source]
        if kind == 2:
            return k_txt_got.at[source]
        if kind == 3:
            return values.at[pl.ds(pl.multiple_of(source * rows, rows), rows)]
        if kind == 4:
            return values.at[pl.ds(pl.multiple_of(all_rows + source * text_rows, text_rows), text_rows)]
        if kind == 5:
            return q_img_got.at[source]
        return q_txt_got.at[source]

    operands = (None, k_img, k_txt, v_img, v_txt, q_img, q_txt)

    def leaving(kind, head):
        if kind == 0:
            return flags_own.at[head]
        return operands[kind].at[:, pl.ds(pl.multiple_of(head * size, size), size)]

    def outward(kind, head):
        return pltpu.make_async_remote_copy(
            src_ref=leaving(kind, head),
            dst_ref=landing(kind, me),
            send_sem=send_sem.at[kind, head],
            recv_sem=recv_sem.at[kind, me],
            device_id={"seq": owner_of(head, heads, odd)},
            device_id_type=pl.DeviceIdType.MESH,
        )

    def inward(kind, source):
        place = landing(kind, source)
        return pltpu.make_async_copy(place, place, recv_sem.at[kind, source])

    for group in ((0, 1, 2), (3, 4), (5, 6)):

        def send_group(step, carry):
            head = lax.rem(step + me, heads)
            target = owner_of(head, heads, odd)

            @pl.when(target != me)
            def _():
                for kind in group:
                    outward(kind, head).start()

            @pl.when(target == me)
            def _():
                for kind in group:
                    pltpu.make_async_copy(
                        leaving(kind, head), landing(kind, me), recv_sem.at[kind, me]
                    ).start()

            return carry

        lax.fori_loop(0, heads, send_group, 0)

    def scaled(block, gain_row):
        floats = block.astype(jnp.float32)
        power = jnp.mean(floats * floats, axis=-1, keepdims=True)
        return floats * lax.rsqrt(power + 1e-06) * gains[gain_row : gain_row + 1, :]

    my_head = head_of(me, heads, odd)
    mine = jnp.logical_and(my_head >= 0, my_head < heads)
    mine = jnp.logical_and(mine, owner_of(my_head, heads, odd) == me)

    def image_copy(chunk, to_section):
        column = pl.multiple_of((section * heads + my_head) * size, size)
        return (
            image_stage.at[chunk, to_section],
            image_out.at[:, pl.ds(column, size)],
        )

    def image_remote(chunk, to_section):
        source, target = image_copy(chunk, to_section)
        return pltpu.make_async_remote_copy(
            src_ref=source,
            dst_ref=target,
            send_sem=image_sent.at[chunk, to_section],
            recv_sem=image_recv.at[section * heads + my_head],
            device_id={"section": to_section, "seq": chunk},
            device_id_type=pl.DeviceIdType.MESH,
        )

    def text_copy(chunk):
        return (
            text_stage.at[chunk],
            text_out.at[:, pl.ds(pl.multiple_of(my_head * size, size), size)],
        )

    def text_remote(chunk):
        source, target = text_copy(chunk)
        return pltpu.make_async_remote_copy(
            src_ref=source,
            dst_ref=target,
            send_sem=text_sent.at[chunk],
            recv_sem=text_recv.at[my_head],
            device_id={"seq": chunk},
            device_id_type=pl.DeviceIdType.MESH,
        )

    @pl.when(mine)
    def _():
        def take_keys(step, carry):
            source = partner(me, step, seqs)
            inward(0, source).wait()
            inward(1, source).wait()
            inward(2, source).wait()
            keys_t[:, pl.ds(pl.multiple_of(source * rows, rows), rows)] = (
                scaled(k_img_got[source], 1).T.astype(jnp.bfloat16)
            )
            return carry

        lax.fori_loop(0, seqs, take_keys, 0)
        text_keys = k_txt_got[...].reshape(seqs * text_rows, size)
        keys_t[:, all_rows:] = scaled(text_keys, 3).T.astype(jnp.bfloat16)

        def take_values(step, carry):
            source = partner(me, step, seqs)
            inward(3, source).wait()
            inward(4, source).wait()
            return carry

        lax.fori_loop(0, seqs, take_values, 0)

        def answer(step, carry):
            chunk = partner(me, step, seqs)
            inward(5, chunk).wait()
            inward(6, chunk).wait()
            queries = jnp.concatenate(
                [scaled(q_img_got[chunk], 0), scaled(q_txt_got[chunk], 2)], axis=0
            ).astype(jnp.bfloat16)
            flags = flags_got[chunk]
            numer = jnp.zeros((rows + text_rows, size), jnp.float32)
            denom = jnp.zeros((rows + text_rows, rows), jnp.float32)
            width = 2 * rows
            for first in range(0, keys_t.shape[1], width):
                scores = jnp.dot(
                    queries, keys_t[:, first : first + width], preferred_element_type=jnp.float32
                )
                weights = jnp.exp2(scores * factor)
                halves = []
                for half in range(2):
                    piece = weights[:, half * rows : (half + 1) * rows]
                    block = first // rows + half
                    if first < all_rows:
                        kept = jnp.where(flags[block : block + 1, :] > 0, piece[:rows], 0.0)
                        piece = jnp.concatenate([kept, piece[rows:]], axis=0)
                    denom = denom + piece
                    halves.append(piece.astype(jnp.bfloat16))
                numer = numer + jnp.dot(
                    jnp.concatenate(halves, axis=1),
                    values[first : first + width, :],
                    preferred_element_type=jnp.float32,
                )
            total[...] = numer / jnp.sum(denom, axis=-1, keepdims=True)
            for to_section in range(sections):
                image_stage[chunk, to_section] = total[
                    pl.ds(to_section, part, stride=sections), :
                ].astype(jnp.bfloat16)
            text_stage[chunk] = total[rows:, :].astype(jnp.bfloat16)
            for to_section in range(sections):
                here = jnp.logical_and(section == to_section, chunk == me)

                @pl.when(jnp.logical_not(here))
                def _():
                    image_remote(chunk, to_section).start()

                @pl.when(here)
                def _():
                    source, target = image_copy(chunk, to_section)
                    pltpu.make_async_copy(
                        source, target, image_recv.at[section * heads + my_head]
                    ).start()

            @pl.when(chunk != me)
            def _():
                text_remote(chunk).start()

            @pl.when(chunk == me)
            def _():
                source, target = text_copy(chunk)
                pltpu.make_async_copy(source, target, text_recv.at[my_head]).start()

            return carry

        lax.fori_loop(0, seqs, answer, 0)

    def finish_group(step, carry):
        head = lax.rem(step + me, heads)

        @pl.when(owner_of(head, heads, odd) != me)
        def _():
            for kind in range(7):
                outward(kind, head).wait_send()

        return carry

    lax.fori_loop(0, heads, finish_group, 0)

    @pl.when(mine)
    def _():
        def sent(chunk, carry):
            for to_section in range(sections):

                @pl.when(jnp.logical_or(section != to_section, chunk != me))
                def _():
                    image_remote(chunk, to_section).wait_send()

            @pl.when(chunk != me)
            def _():
                text_remote(chunk).wait_send()

            return carry

        lax.fori_loop(0, seqs, sent, 0)

    def arrived(head, carry):
        place = image_out.at[:, pl.ds(pl.multiple_of(head * size, size), size)]
        pltpu.make_async_copy(place, place, image_recv.at[head]).wait()
        return carry

    lax.fori_loop(0, sections * heads, arrived, 0)

    def text_arrived(head, carry):
        place = text_out.at[:, pl.ds(pl.multiple_of(head * size, size), size)]
        pltpu.make_async_copy(place, place, text_recv.at[head]).wait()
        return carry

    lax.fori_loop(0, heads, text_arrived, 0)


def by_heads(q_img, k_img, v_img, q_txt, k_txt, v_txt, norm_gains, block_map):
    rows, width = q_img.shape
    size = norm_gains.shape[1]
    heads = width // size
    text_rows = q_txt.shape[0]
    seqs = lax.axis_size("seq")
    sections = lax.axis_size("section")
    half = jnp.bfloat16
    flags_shape = (block_map.shape[2], size)
    anywhere = pl.BlockSpec(memory_space=pl.ANY)
    dma = pltpu.SemaphoreType.DMA
    image_flat, text_out = pl.pallas_call(
        functools.partial(head_kernel, heads, seqs, sections),
        out_shape=(
            jax.ShapeDtypeStruct((rows // sections, sections * width), half),
            jax.ShapeDtypeStruct((text_rows, width), half),
        ),
        in_specs=[anywhere] * 6
        + [pl.BlockSpec(memory_space=pltpu.VMEM), pl.BlockSpec(memory_space=pltpu.SMEM)],
        out_specs=(anywhere, anywhere),
        scratch_shapes=[
            pltpu.VMEM((heads,) + flags_shape, jnp.int32),
            pltpu.VMEM((seqs,) + flags_shape, jnp.int32),
            pltpu.VMEM((seqs, rows, size), half),
            pltpu.VMEM((seqs, text_rows, size), half),
            pltpu.VMEM((seqs, rows, size), half),
            pltpu.VMEM((seqs, text_rows, size), half),
            pltpu.VMEM((seqs * (rows + text_rows), size), half),
            pltpu.VMEM((size, seqs * (rows + text_rows)), half),
            pltpu.VMEM((rows + text_rows, size), jnp.float32),
            pltpu.VMEM((seqs, sections, rows // sections, size), half),
            pltpu.VMEM((seqs, text_rows, size), half),
            dma((7, heads)),
            dma((7, seqs)),
            dma((seqs, sections)),
            dma((seqs,)),
            dma((sections * heads,)),
            dma((heads,)),
        ],
        compiler_params=pltpu.CompilerParams(
            collective_id=0, has_side_effects=True, vmem_limit_bytes=32 * 1024 * 1024
        ),
    )(q_img, k_img, v_img, q_txt, k_txt, v_txt, norm_gains, block_map)
    return (image_flat.reshape(rows // sections, 1, sections * width), text_out)


def one_head_fits(rows, text_rows, heads, head_size, key_blocks, seqs, sections):
    return (
        rows == BLOCK
        and head_size == BLOCK
        and seqs == heads + 2
        and seqs & (seqs - 1) == 0
        and key_blocks == seqs
        and seqs % 8 == 0
        and text_rows % 16 == 0
        and (seqs * text_rows) % (2 * BLOCK) == 0
        and rows % (16 * sections) == 0
        and sections % 2 == 0
    )


def layer(q_img, k_img, v_img, q_txt, k_txt, v_txt, norm_gains, block_map):
    rows, width = q_img.shape
    head_size = norm_gains.shape[1]
    fits = one_head_fits(
        rows,
        q_txt.shape[0],
        width // head_size,
        head_size,
        block_map.shape[2],
        lax.axis_size("seq"),
        lax.axis_size("section"),
    )
    chosen = by_heads if fits else body
    return chosen(q_img, k_img, v_img, q_txt, k_txt, v_txt, norm_gains, block_map)


def solution(mesh):
    placed = (
        P("seq", "section"),
        P("seq", "section"),
        P("seq", "section"),
        P("seq", "section"),
        P("seq", "section"),
        P("seq", "section"),
        P(),
        P("section", "seq", None),
    )
    return jax.shard_map(
        layer,
        mesh=mesh,
        in_specs=placed,
        out_specs=(P("seq", "section", None), P("seq", "section")),
        check_vma=False,
    )
```

```python
import functools
import math

import jax
import jax.numpy as jnp
from jax import lax
from jax.experimental import pallas as pl
from jax.experimental.pallas import tpu as pltpu
from jax.sharding import PartitionSpec as P

BLOCK = 128


def normed(values, gain, heads):
    rows = values.shape[0]
    floats = values.astype(jnp.float32).reshape(rows, heads, gain.shape[0])
    power = jnp.mean(floats * floats, axis=-1, keepdims=True)
    return (floats * lax.rsqrt(power + 1e-06) * gain).astype(jnp.bfloat16)


def make_keep(flags, query_shards, shards, first, rows, text_rows):
    heads = flags.shape[0]
    key_blocks = rows // BLOCK
    stride = rows + text_rows
    picked = lax.dynamic_slice_in_dim(flags, first * key_blocks, shards * key_blocks, 2)
    picked = picked.reshape(heads, query_shards, key_blocks, shards, key_blocks)
    image_mask = jnp.broadcast_to(
        picked[:, :, :, None, :, :, None] > 0,
        (heads, query_shards, key_blocks, BLOCK, shards, key_blocks, BLOCK),
    )
    image_mask = image_mask.reshape(heads, query_shards, rows, shards, rows)
    keep = jnp.pad(
        image_mask, ((0, 0), (0, 0), (0, text_rows), (0, 0), (0, text_rows)), constant_values=True
    )
    return keep.reshape(heads, query_shards * stride, shards, stride)


def accumulate(queries, flags, query_shards, rows, text_rows, carry, pieces, start):
    numer, denom = carry
    piece_keys, piece_values = pieces
    heads = queries.shape[1]
    head_size = queries.shape[2]
    stride = rows + text_rows
    shards = piece_keys.shape[0] // stride
    first = start // stride
    keys_four = piece_keys.reshape(shards, stride, heads, head_size)
    values_four = piece_values.reshape(shards, stride, heads, head_size)
    scores = jnp.einsum(
        "qhd,skhd->hqsk", queries, keys_four, preferred_element_type=jnp.float32
    ) * head_size ** (-0.5)
    keep = make_keep(flags, query_shards, shards, first, rows, text_rows)
    weights = jnp.where(keep, jnp.exp(scores), jnp.float32(0.0))
    denom = denom + jnp.sum(weights, axis=(2, 3))
    numer = numer + jnp.einsum(
        "hqsk,skhd->hqd",
        weights.astype(jnp.bfloat16),
        values_four,
        preferred_element_type=jnp.float32,
    )
    return (numer, denom)


def body(q_img, k_img, v_img, q_txt, k_txt, v_txt, norm_gains, block_map):
    rows, width = q_img.shape
    head_size = norm_gains.shape[1]
    heads = width // head_size
    text_rows = q_txt.shape[0]
    stride = rows + text_rows
    queries = jnp.concatenate(
        [normed(q_img, norm_gains[0], heads), normed(q_txt, norm_gains[2], heads)], axis=0
    )
    keys_image = normed(k_img, norm_gains[1], heads).reshape(rows, width)
    keys_text = normed(k_txt, norm_gains[3], heads).reshape(text_rows, width)
    local_keys = jnp.concatenate([keys_image, keys_text], axis=0)
    local_values = jnp.concatenate([v_img, v_txt], axis=0)
    start_state = (
        jnp.zeros((heads, stride, head_size), jnp.float32),
        jnp.zeros((heads, stride), jnp.float32),
    )

    def fold_step(carry, pieces, start):
        return accumulate(queries, block_map, 1, rows, text_rows, carry, pieces, start)

    whole_keys, whole_values = (
        lax.all_gather(local_keys, "seq", axis=0, tiled=True),
        lax.all_gather(local_values, "seq", axis=0, tiled=True),
    )
    count_seq = lax.axis_size("seq")
    grouped = 1
    while (
        grouped * 2 <= count_seq
        and count_seq % (grouped * 2) == 0
        and (grouped * 2 * stride <= 1024)
    ):
        grouped = grouped * 2
    span = grouped * stride

    def step_over(index, carry):
        offset = index * span
        piece_keys = lax.dynamic_slice_in_dim(whole_keys, offset, span, 0)
        piece_values = lax.dynamic_slice_in_dim(whole_values, offset, span, 0)
        return fold_step(carry, (piece_keys, piece_values), offset)

    numer, denom = lax.fori_loop(0, count_seq // grouped, step_over, start_state)
    result = numer / denom[..., None]
    merged = result.transpose(1, 0, 2).reshape(stride, width).astype(jnp.bfloat16)
    image_part = merged[:rows]
    text_out = merged[rows:]
    sections = lax.axis_size("section")
    image_out = lax.all_to_all(
        image_part.reshape(rows // sections, sections, width),
        "section",
        split_axis=1,
        concat_axis=2,
        tiled=True,
    )
    return (image_out, text_out)


def owner_of(head, heads, odd):
    even_pick = head + lax.div(head + heads - 2, heads - 1) + lax.div(head, heads - 1)
    return odd * (head + 1) + (1 - odd) * even_pick


def head_of(place, heads, odd):
    last = heads + 1
    even_pick = place - lax.div(place + last - 1, last) - lax.div(place, last)
    return odd * (place - 1) + (1 - odd) * even_pick


def partner(place, step, count):
    total = 0
    bit = 1
    while bit < count:
        total = total + bit * lax.rem(lax.div(place, bit) + lax.div(step, bit), 2)
        bit *= 2
    return total


def head_kernel(
    heads, seqs, sections,
    q_img, k_img, v_img, q_txt, k_txt, v_txt, gains, flags_in,
    image_out, text_out,
    flags_own, flags_got, q_img_got, q_txt_got, k_img_got, k_txt_got, values, keys_t, total,
    image_stage, text_stage,
    send_sem, recv_sem, image_sent, text_sent, image_recv, text_recv,
):
    rows = q_img.shape[0]
    text_rows = q_txt.shape[0]
    size = gains.shape[1]
    key_blocks = flags_in.shape[2]
    part = rows // sections
    all_rows = seqs * rows
    factor = size ** (-0.5) * math.log2(math.e)
    section = lax.axis_index("section")
    me = lax.axis_index("seq")
    odd = lax.rem(section, 2)

    barrier = pltpu.get_barrier_semaphore()

    def greet(index, carry):
        to_section = lax.div(index, seqs)
        to_seq = lax.rem(index, seqs)

        @pl.when(jnp.logical_or(to_section != section, to_seq != me))
        def _():
            pl.semaphore_signal(
                barrier,
                inc=1,
                device_id={"section": to_section, "seq": to_seq},
                device_id_type=pl.DeviceIdType.MESH,
            )

        return carry

    lax.fori_loop(0, sections * seqs, greet, 0)
    for head in range(heads):
        for block in range(key_blocks):
            flags_own[head, block : block + 1, :] = jnp.full(
                (1, flags_own.shape[2]), flags_in[head, 0, block], jnp.int32
            )
    pl.semaphore_wait(barrier, sections * seqs - 1)

    def landing(kind, source):
        if kind == 0:
            return flags_got.at[source]
        if kind == 1:
            return k_img_got.at[source]
        if kind == 2:
            return k_txt_got.at[source]
        if kind == 3:
            return values.at[pl.ds(pl.multiple_of(source * rows, rows), rows)]
        if kind == 4:
            return values.at[pl.ds(pl.multiple_of(all_rows + source * text_rows, text_rows), text_rows)]
        if kind == 5:
            return q_img_got.at[source]
        return q_txt_got.at[source]

    operands = (None, k_img, k_txt, v_img, v_txt, q_img, q_txt)

    def leaving(kind, head):
        if kind == 0:
            return flags_own.at[head]
        return operands[kind].at[:, pl.ds(pl.multiple_of(head * size, size), size)]

    def outward(kind, head):
        return pltpu.make_async_remote_copy(
            src_ref=leaving(kind, head),
            dst_ref=landing(kind, me),
            send_sem=send_sem.at[kind, head],
            recv_sem=recv_sem.at[kind, me],
            device_id={"seq": owner_of(head, heads, odd)},
            device_id_type=pl.DeviceIdType.MESH,
        )

    def inward(kind, source):
        place = landing(kind, source)
        return pltpu.make_async_copy(place, place, recv_sem.at[kind, source])

    for group in ((0, 1, 2), (3, 4), (5, 6)):

        def send_group(step, carry):
            head = lax.rem(step + me, heads)
            target = owner_of(head, heads, odd)

            @pl.when(target != me)
            def _():
                for kind in group:
                    outward(kind, head).start()

            @pl.when(target == me)
            def _():
                for kind in group:
                    pltpu.make_async_copy(
                        leaving(kind, head), landing(kind, me), recv_sem.at[kind, me]
                    ).start()

            return carry

        lax.fori_loop(0, heads, send_group, 0)

    def scaled(block, gain_row):
        floats = block.astype(jnp.float32)
        power = jnp.mean(floats * floats, axis=-1, keepdims=True)
        return floats * lax.rsqrt(power + 1e-06) * gains[gain_row : gain_row + 1, :]

    my_head = head_of(me, heads, odd)
    mine = jnp.logical_and(my_head >= 0, my_head < heads)
    mine = jnp.logical_and(mine, owner_of(my_head, heads, odd) == me)

    def image_copy(chunk, to_section):
        column = pl.multiple_of((section * heads + my_head) * size, size)
        return (
            image_stage.at[chunk, to_section],
            image_out.at[:, pl.ds(column, size)],
        )

    def image_remote(chunk, to_section):
        source, target = image_copy(chunk, to_section)
        return pltpu.make_async_remote_copy(
            src_ref=source,
            dst_ref=target,
            send_sem=image_sent.at[chunk, to_section],
            recv_sem=image_recv.at[section * heads + my_head],
            device_id={"section": to_section, "seq": chunk},
            device_id_type=pl.DeviceIdType.MESH,
        )

    def text_copy(chunk):
        return (
            text_stage.at[chunk],
            text_out.at[:, pl.ds(pl.multiple_of(my_head * size, size), size)],
        )

    def text_remote(chunk):
        source, target = text_copy(chunk)
        return pltpu.make_async_remote_copy(
            src_ref=source,
            dst_ref=target,
            send_sem=text_sent.at[chunk],
            recv_sem=text_recv.at[my_head],
            device_id={"seq": chunk},
            device_id_type=pl.DeviceIdType.MESH,
        )

    @pl.when(mine)
    def _():
        def take_keys(step, carry):
            source = partner(me, step, seqs)
            inward(0, source).wait()
            inward(1, source).wait()
            inward(2, source).wait()
            keys_t[:, pl.ds(pl.multiple_of(source * rows, rows), rows)] = (
                scaled(k_img_got[source], 1).T.astype(jnp.bfloat16)
            )
            return carry

        lax.fori_loop(0, seqs, take_keys, 0)
        text_keys = k_txt_got[...].reshape(seqs * text_rows, size)
        keys_t[:, all_rows:] = scaled(text_keys, 3).T.astype(jnp.bfloat16)

        def take_values(step, carry):
            source = partner(me, step, seqs)
            inward(3, source).wait()
            inward(4, source).wait()
            return carry

        lax.fori_loop(0, seqs, take_values, 0)

        def answer(step, carry):
            chunk = partner(me, step, seqs)
            inward(5, chunk).wait()
            inward(6, chunk).wait()
            queries = jnp.concatenate(
                [scaled(q_img_got[chunk], 0), scaled(q_txt_got[chunk], 2)], axis=0
            ).astype(jnp.bfloat16)
            flags = flags_got[chunk]
            numer = jnp.zeros((rows + text_rows, size), jnp.float32)
            denom = jnp.zeros((rows + text_rows, rows), jnp.float32)
            width = 2 * rows
            for first in range(0, keys_t.shape[1], width):
                scores = jnp.dot(
                    queries, keys_t[:, first : first + width], preferred_element_type=jnp.float32
                )
                weights = jnp.exp2(scores * factor)
                halves = []
                for half in range(2):
                    piece = weights[:, half * rows : (half + 1) * rows]
                    block = first // rows + half
                    if first < all_rows:
                        kept = jnp.where(flags[block : block + 1, :] > 0, piece[:rows], 0.0)
                        piece = jnp.concatenate([kept, piece[rows:]], axis=0)
                    denom = denom + piece
                    halves.append(piece.astype(jnp.bfloat16))
                numer = numer + jnp.dot(
                    jnp.concatenate(halves, axis=1),
                    values[first : first + width, :],
                    preferred_element_type=jnp.float32,
                )
            total[...] = numer / jnp.sum(denom, axis=-1, keepdims=True)
            for to_section in range(sections):
                image_stage[chunk, to_section] = total[
                    pl.ds(to_section, part, stride=sections), :
                ].astype(jnp.bfloat16)
            text_stage[chunk] = total[rows:, :].astype(jnp.bfloat16)
            for to_section in range(sections):
                here = jnp.logical_and(section == to_section, chunk == me)

                @pl.when(jnp.logical_not(here))
                def _():
                    image_remote(chunk, to_section).start()

                @pl.when(here)
                def _():
                    source, target = image_copy(chunk, to_section)
                    pltpu.make_async_copy(
                        source, target, image_recv.at[section * heads + my_head]
                    ).start()

            @pl.when(chunk != me)
            def _():
                text_remote(chunk).start()

            @pl.when(chunk == me)
            def _():
                source, target = text_copy(chunk)
                pltpu.make_async_copy(source, target, text_recv.at[my_head]).start()

            return carry

        lax.fori_loop(0, seqs, answer, 0)

    def finish_group(step, carry):
        head = lax.rem(step + me, heads)

        @pl.when(owner_of(head, heads, odd) != me)
        def _():
            for kind in range(7):
                outward(kind, head).wait_send()

        return carry

    lax.fori_loop(0, heads, finish_group, 0)

    @pl.when(mine)
    def _():
        def sent(chunk, carry):
            for to_section in range(sections):

                @pl.when(jnp.logical_or(section != to_section, chunk != me))
                def _():
                    image_remote(chunk, to_section).wait_send()

            @pl.when(chunk != me)
            def _():
                text_remote(chunk).wait_send()

            return carry

        lax.fori_loop(0, seqs, sent, 0)

    def arrived(head, carry):
        place = image_out.at[:, pl.ds(pl.multiple_of(head * size, size), size)]
        pltpu.make_async_copy(place, place, image_recv.at[head]).wait()
        return carry

    lax.fori_loop(0, sections * heads, arrived, 0)

    def text_arrived(head, carry):
        place = text_out.at[:, pl.ds(pl.multiple_of(head * size, size), size)]
        pltpu.make_async_copy(place, place, text_recv.at[head]).wait()
        return carry

    lax.fori_loop(0, heads, text_arrived, 0)


def by_heads(q_img, k_img, v_img, q_txt, k_txt, v_txt, norm_gains, block_map):
    rows, width = q_img.shape
    size = norm_gains.shape[1]
    heads = width // size
    text_rows = q_txt.shape[0]
    seqs = lax.axis_size("seq")
    sections = lax.axis_size("section")
    half = jnp.bfloat16
    flags_shape = (block_map.shape[2], size)
    anywhere = pl.BlockSpec(memory_space=pl.ANY)
    dma = pltpu.SemaphoreType.DMA
    image_flat, text_out = pl.pallas_call(
        functools.partial(head_kernel, heads, seqs, sections),
        out_shape=(
            jax.ShapeDtypeStruct((rows // sections, sections * width), half),
            jax.ShapeDtypeStruct((text_rows, width), half),
        ),
        in_specs=[anywhere] * 6
        + [pl.BlockSpec(memory_space=pltpu.VMEM), pl.BlockSpec(memory_space=pltpu.SMEM)],
        out_specs=(anywhere, anywhere),
        scratch_shapes=[
            pltpu.VMEM((heads,) + flags_shape, jnp.int32),
            pltpu.VMEM((seqs,) + flags_shape, jnp.int32),
            pltpu.VMEM((seqs, rows, size), half),
            pltpu.VMEM((seqs, text_rows, size), half),
            pltpu.VMEM((seqs, rows, size), half),
            pltpu.VMEM((seqs, text_rows, size), half),
            pltpu.VMEM((seqs * (rows + text_rows), size), half),
            pltpu.VMEM((size, seqs * (rows + text_rows)), half),
            pltpu.VMEM((rows + text_rows, size), jnp.float32),
            pltpu.VMEM((seqs, sections, rows // sections, size), half),
            pltpu.VMEM((seqs, text_rows, size), half),
            dma((7, heads)),
            dma((7, seqs)),
            dma((seqs, sections)),
            dma((seqs,)),
            dma((sections * heads,)),
            dma((heads,)),
        ],
        compiler_params=pltpu.CompilerParams(
            collective_id=0, has_side_effects=True, vmem_limit_bytes=60 * 1024 * 1024
        ),
    )(q_img, k_img, v_img, q_txt, k_txt, v_txt, norm_gains, block_map)
    return (image_flat.reshape(rows // sections, 1, sections * width), text_out)


def one_head_fits(rows, text_rows, heads, head_size, key_blocks, seqs, sections):
    return (
        rows == BLOCK
        and head_size == BLOCK
        and seqs == heads + 2
        and seqs & (seqs - 1) == 0
        and key_blocks == seqs
        and seqs % 8 == 0
        and text_rows % 16 == 0
        and (seqs * text_rows) % (2 * BLOCK) == 0
        and rows % (16 * sections) == 0
        and sections % 2 == 0
    )


def layer(q_img, k_img, v_img, q_txt, k_txt, v_txt, norm_gains, block_map):
    rows, width = q_img.shape
    head_size = norm_gains.shape[1]
    fits = one_head_fits(
        rows,
        q_txt.shape[0],
        width // head_size,
        head_size,
        block_map.shape[2],
        lax.axis_size("seq"),
        lax.axis_size("section"),
    )
    chosen = by_heads if fits else body
    return chosen(q_img, k_img, v_img, q_txt, k_txt, v_txt, norm_gains, block_map)


def solution(mesh):
    placed = (
        P("seq", "section"),
        P("seq", "section"),
        P("seq", "section"),
        P("seq", "section"),
        P("seq", "section"),
        P("seq", "section"),
        P(),
        P("section", "seq", None),
    )
    return jax.shard_map(
        layer,
        mesh=mesh,
        in_specs=placed,
        out_specs=(P("seq", "section", None), P("seq", "section")),
        check_vma=False,
    )
```

```python
import functools
import math

import jax
import jax.numpy as jnp
from jax import lax
from jax.experimental import pallas as pl
from jax.experimental.pallas import tpu as pltpu
from jax.sharding import PartitionSpec as P

BLOCK = 128


def normed(values, gain, heads):
    rows = values.shape[0]
    floats = values.astype(jnp.float32).reshape(rows, heads, gain.shape[0])
    power = jnp.mean(floats * floats, axis=-1, keepdims=True)
    return (floats * lax.rsqrt(power + 1e-06) * gain).astype(jnp.bfloat16)


def make_keep(flags, query_shards, shards, first, rows, text_rows):
    heads = flags.shape[0]
    key_blocks = rows // BLOCK
    stride = rows + text_rows
    picked = lax.dynamic_slice_in_dim(flags, first * key_blocks, shards * key_blocks, 2)
    picked = picked.reshape(heads, query_shards, key_blocks, shards, key_blocks)
    image_mask = jnp.broadcast_to(
        picked[:, :, :, None, :, :, None] > 0,
        (heads, query_shards, key_blocks, BLOCK, shards, key_blocks, BLOCK),
    )
    image_mask = image_mask.reshape(heads, query_shards, rows, shards, rows)
    keep = jnp.pad(
        image_mask, ((0, 0), (0, 0), (0, text_rows), (0, 0), (0, text_rows)), constant_values=True
    )
    return keep.reshape(heads, query_shards * stride, shards, stride)


def accumulate(queries, flags, query_shards, rows, text_rows, carry, pieces, start):
    numer, denom = carry
    piece_keys, piece_values = pieces
    heads = queries.shape[1]
    head_size = queries.shape[2]
    stride = rows + text_rows
    shards = piece_keys.shape[0] // stride
    first = start // stride
    keys_four = piece_keys.reshape(shards, stride, heads, head_size)
    values_four = piece_values.reshape(shards, stride, heads, head_size)
    scores = jnp.einsum(
        "qhd,skhd->hqsk", queries, keys_four, preferred_element_type=jnp.float32
    ) * head_size ** (-0.5)
    keep = make_keep(flags, query_shards, shards, first, rows, text_rows)
    weights = jnp.where(keep, jnp.exp(scores), jnp.float32(0.0))
    denom = denom + jnp.sum(weights, axis=(2, 3))
    numer = numer + jnp.einsum(
        "hqsk,skhd->hqd",
        weights.astype(jnp.bfloat16),
        values_four,
        preferred_element_type=jnp.float32,
    )
    return (numer, denom)


def body(q_img, k_img, v_img, q_txt, k_txt, v_txt, norm_gains, block_map):
    rows, width = q_img.shape
    head_size = norm_gains.shape[1]
    heads = width // head_size
    text_rows = q_txt.shape[0]
    stride = rows + text_rows
    queries = jnp.concatenate(
        [normed(q_img, norm_gains[0], heads), normed(q_txt, norm_gains[2], heads)], axis=0
    )
    keys_image = normed(k_img, norm_gains[1], heads).reshape(rows, width)
    keys_text = normed(k_txt, norm_gains[3], heads).reshape(text_rows, width)
    local_keys = jnp.concatenate([keys_image, keys_text], axis=0)
    local_values = jnp.concatenate([v_img, v_txt], axis=0)
    start_state = (
        jnp.zeros((heads, stride, head_size), jnp.float32),
        jnp.zeros((heads, stride), jnp.float32),
    )

    def fold_step(carry, pieces, start):
        return accumulate(queries, block_map, 1, rows, text_rows, carry, pieces, start)

    whole_keys, whole_values = (
        lax.all_gather(local_keys, "seq", axis=0, tiled=True),
        lax.all_gather(local_values, "seq", axis=0, tiled=True),
    )
    count_seq = lax.axis_size("seq")
    grouped = 1
    while (
        grouped * 2 <= count_seq
        and count_seq % (grouped * 2) == 0
        and (grouped * 2 * stride <= 1024)
    ):
        grouped = grouped * 2
    span = grouped * stride

    def step_over(index, carry):
        offset = index * span
        piece_keys = lax.dynamic_slice_in_dim(whole_keys, offset, span, 0)
        piece_values = lax.dynamic_slice_in_dim(whole_values, offset, span, 0)
        return fold_step(carry, (piece_keys, piece_values), offset)

    numer, denom = lax.fori_loop(0, count_seq // grouped, step_over, start_state)
    result = numer / denom[..., None]
    merged = result.transpose(1, 0, 2).reshape(stride, width).astype(jnp.bfloat16)
    image_part = merged[:rows]
    text_out = merged[rows:]
    sections = lax.axis_size("section")
    image_out = lax.all_to_all(
        image_part.reshape(rows // sections, sections, width),
        "section",
        split_axis=1,
        concat_axis=2,
        tiled=True,
    )
    return (image_out, text_out)


def owner_of(head):
    return head + 1


def partner(place, step, count):
    total = 0
    bit = 1
    while bit < count:
        total = total + bit * lax.rem(lax.div(place, bit) + lax.div(step, bit), 2)
        bit *= 2
    return total


def head_kernel(
    heads, seqs, sections,
    q_img, k_img, v_img, q_txt, k_txt, v_txt, gains, flags_in,
    image_out, text_out,
    flags_own, flags_got, q_got, k_got, v_got, values, keys_t, total,
    image_stage, text_stage,
    held_q, held_k, held_v,
    send_sem, recv_sem, image_sent, text_sent, image_recv, text_recv, ready, load_sem,
):
    rows = q_img.shape[0]
    text_rows = q_txt.shape[0]
    size = gains.shape[1]
    key_blocks = flags_in.shape[2]
    part = rows // sections
    all_rows = seqs * rows
    factor = size ** (-0.5) * math.log2(math.e)
    section = lax.axis_index("section")
    me = lax.axis_index("seq")

    near = heads // 2

    barrier = pltpu.get_barrier_semaphore()

    loads = [
        pltpu.make_async_copy(source, target, load_sem.at[index])
        for index, (source, target) in enumerate(
            (
                (k_img, held_k.at[:rows]),
                (k_txt, held_k.at[rows:]),
                (v_img, held_v.at[:rows]),
                (v_txt, held_v.at[rows:]),
                (q_img, held_q.at[:rows]),
                (q_txt, held_q.at[rows:]),
            )
        )
    ]

    def signal(semaphore, **place):
        pl.semaphore_signal(
            semaphore, inc=1, device_id=place, device_id_type=pl.DeviceIdType.MESH
        )

    for step in range(1, seqs):
        signal(barrier, seq=lax.rem(me + step, seqs))
    for step in range(1, sections):
        signal(barrier, section=lax.rem(section + step, sections))
    for load in loads:
        load.start()
    for head in range(heads):
        for block in range(key_blocks):
            flags_own[head, block : block + 1, :] = jnp.full(
                (1, flags_own.shape[2]), flags_in[head, 0, block], jnp.int32
            )
    pl.semaphore_wait(barrier, sections + seqs - 2)
    for step in range(1, sections):
        signal(ready, section=lax.rem(section + step, sections))

    def landing(kind, source):
        if kind == 0:
            return flags_got.at[source]
        return (k_got, v_got, q_got)[kind - 1].at[source]

    operands = (None, held_k, held_v, held_q)

    def leaving(kind, head):
        if kind == 0:
            return flags_own.at[head]
        return operands[kind].at[:, pl.ds(pl.multiple_of(head * size, size), size)]

    def outward(kind, head):
        return pltpu.make_async_remote_copy(
            src_ref=leaving(kind, head),
            dst_ref=landing(kind, me),
            send_sem=send_sem.at[kind, head],
            recv_sem=recv_sem.at[kind, me],
            device_id={"seq": owner_of(head)},
            device_id_type=pl.DeviceIdType.MESH,
        )

    def inward(kind, source):
        place = landing(kind, source)
        return pltpu.make_async_copy(place, place, recv_sem.at[kind, source])

    for group in ((0, 1), (2,), (3,)):
        for kind in group:
            if kind > 0:
                loads[2 * kind - 2].wait()
                loads[2 * kind - 1].wait()

        def send_group(step, carry):
            turn = lax.rem(lax.div(step, near) + 1 - lax.div(me, seqs // 2), 2)
            head = turn * near + lax.rem(step + me, near)
            target = owner_of(head)

            @pl.when(target != me)
            def _():
                for kind in group:
                    outward(kind, head).start()

            @pl.when(target == me)
            def _():
                for kind in group:
                    pltpu.make_async_copy(
                        leaving(kind, head), landing(kind, me), recv_sem.at[kind, me]
                    ).start()

            return carry

        lax.fori_loop(0, heads, send_group, 0)

    def scaled(block, gain_row):
        floats = block.astype(jnp.float32)
        power = jnp.mean(floats * floats, axis=-1, keepdims=True)
        return floats * lax.rsqrt(power + 1e-06) * gains[gain_row : gain_row + 1, :]

    my_head = me - 1
    mine = jnp.logical_and(my_head >= 0, my_head < heads)

    def image_copy(chunk, to_section):
        column = pl.multiple_of((section * heads + my_head) * size, size)
        return (
            image_stage.at[chunk, to_section],
            image_out.at[:, pl.ds(column, size)],
        )

    def image_remote(chunk, to_section):
        source, target = image_copy(chunk, to_section)
        return pltpu.make_async_remote_copy(
            src_ref=source,
            dst_ref=target,
            send_sem=image_sent.at[chunk, to_section],
            recv_sem=image_recv.at[section * heads + my_head],
            device_id={"section": to_section, "seq": chunk},
            device_id_type=pl.DeviceIdType.MESH,
        )

    def text_copy(chunk):
        return (
            text_stage.at[chunk],
            text_out.at[:, pl.ds(pl.multiple_of(my_head * size, size), size)],
        )

    def text_remote(chunk):
        source, target = text_copy(chunk)
        return pltpu.make_async_remote_copy(
            src_ref=source,
            dst_ref=target,
            send_sem=text_sent.at[chunk],
            recv_sem=text_recv.at[my_head],
            device_id={"seq": chunk},
            device_id_type=pl.DeviceIdType.MESH,
        )

    pl.semaphore_wait(ready, sections - 1)

    @pl.when(mine)
    def _():
        def take_keys(step, carry):
            source = partner(me, step, seqs)
            inward(0, source).wait()
            inward(1, source).wait()
            keys_t[:, pl.ds(pl.multiple_of(source * rows, rows), rows)] = (
                scaled(k_got[source, :rows], 1).T.astype(jnp.bfloat16)
            )
            return carry

        lax.fori_loop(0, seqs, take_keys, 0)
        text_keys = k_got[:, rows:].reshape(seqs * text_rows, size)
        keys_t[:, all_rows:] = scaled(text_keys, 3).T.astype(jnp.bfloat16)

        def take_values(step, carry):
            source = partner(me, step, seqs)
            inward(2, source).wait()
            image_place = pl.ds(pl.multiple_of(source * rows, rows), rows)
            values[image_place, :] = v_got[source, :rows]
            text_place = pl.multiple_of(all_rows + source * text_rows, text_rows)
            values[pl.ds(text_place, text_rows), :] = v_got[source, rows:]
            return carry

        lax.fori_loop(0, seqs, take_values, 0)

        def answer(step, carry):
            chunk = partner(me, step, seqs)
            inward(3, chunk).wait()
            queries = jnp.concatenate(
                [scaled(q_got[chunk, :rows], 0), scaled(q_got[chunk, rows:], 2)], axis=0
            ).astype(jnp.bfloat16)
            flags = flags_got[chunk]
            numer = jnp.zeros((rows + text_rows, size), jnp.float32)
            denom = jnp.zeros((rows + text_rows, rows), jnp.float32)
            width = 2 * rows
            for first in range(0, keys_t.shape[1], width):
                scores = jnp.dot(
                    queries, keys_t[:, first : first + width], preferred_element_type=jnp.float32
                )
                weights = jnp.exp2(scores * factor)
                halves = []
                for half in range(2):
                    piece = weights[:, half * rows : (half + 1) * rows]
                    block = first // rows + half
                    if first < all_rows:
                        kept = jnp.where(flags[block : block + 1, :] > 0, piece[:rows], 0.0)
                        piece = jnp.concatenate([kept, piece[rows:]], axis=0)
                    denom = denom + piece
                    halves.append(piece.astype(jnp.bfloat16))
                numer = numer + jnp.dot(
                    jnp.concatenate(halves, axis=1),
                    values[first : first + width, :],
                    preferred_element_type=jnp.float32,
                )
            total[...] = numer / jnp.sum(denom, axis=-1, keepdims=True)
            for to_section in range(sections):
                image_stage[chunk, to_section] = total[
                    pl.ds(to_section, part, stride=sections), :
                ].astype(jnp.bfloat16)
            text_stage[chunk] = total[rows:, :].astype(jnp.bfloat16)
            for to_section in range(sections):
                here = jnp.logical_and(section == to_section, chunk == me)

                @pl.when(jnp.logical_not(here))
                def _():
                    image_remote(chunk, to_section).start()

                @pl.when(here)
                def _():
                    source, target = image_copy(chunk, to_section)
                    pltpu.make_async_copy(
                        source, target, image_recv.at[section * heads + my_head]
                    ).start()

            @pl.when(chunk != me)
            def _():
                text_remote(chunk).start()

            @pl.when(chunk == me)
            def _():
                source, target = text_copy(chunk)
                pltpu.make_async_copy(source, target, text_recv.at[my_head]).start()

            return carry

        lax.fori_loop(0, seqs, answer, 0)

    def finish_group(step, carry):
        head = lax.rem(step + me, heads)

        @pl.when(owner_of(head) != me)
        def _():
            for kind in range(4):
                outward(kind, head).wait_send()

        return carry

    lax.fori_loop(0, heads, finish_group, 0)

    @pl.when(mine)
    def _():
        def sent(chunk, carry):
            for to_section in range(sections):

                @pl.when(jnp.logical_or(section != to_section, chunk != me))
                def _():
                    image_remote(chunk, to_section).wait_send()

            @pl.when(chunk != me)
            def _():
                text_remote(chunk).wait_send()

            return carry

        lax.fori_loop(0, seqs, sent, 0)

    def arrived(head, carry):
        place = image_out.at[:, pl.ds(pl.multiple_of(head * size, size), size)]
        pltpu.make_async_copy(place, place, image_recv.at[head]).wait()
        return carry

    lax.fori_loop(0, sections * heads, arrived, 0)

    def text_arrived(head, carry):
        place = text_out.at[:, pl.ds(pl.multiple_of(head * size, size), size)]
        pltpu.make_async_copy(place, place, text_recv.at[head]).wait()
        return carry

    lax.fori_loop(0, heads, text_arrived, 0)


def by_heads(q_img, k_img, v_img, q_txt, k_txt, v_txt, norm_gains, block_map):
    rows, width = q_img.shape
    size = norm_gains.shape[1]
    heads = width // size
    text_rows = q_txt.shape[0]
    seqs = lax.axis_size("seq")
    sections = lax.axis_size("section")
    half = jnp.bfloat16
    flags_shape = (block_map.shape[2], size)
    anywhere = pl.BlockSpec(memory_space=pl.ANY)
    dma = pltpu.SemaphoreType.DMA
    image_flat, text_out = pl.pallas_call(
        functools.partial(head_kernel, heads, seqs, sections),
        out_shape=(
            jax.ShapeDtypeStruct((rows // sections, sections * width), half),
            jax.ShapeDtypeStruct((text_rows, width), half),
        ),
        in_specs=[anywhere] * 6
        + [pl.BlockSpec(memory_space=pltpu.VMEM), pl.BlockSpec(memory_space=pltpu.SMEM)],
        out_specs=(anywhere, anywhere),
        scratch_shapes=[
            pltpu.VMEM((heads,) + flags_shape, jnp.int32),
            pltpu.VMEM((seqs,) + flags_shape, jnp.int32),
            pltpu.VMEM((seqs, rows + text_rows, size), half),
            pltpu.VMEM((seqs, rows + text_rows, size), half),
            pltpu.VMEM((seqs, rows + text_rows, size), half),
            pltpu.VMEM((seqs * (rows + text_rows), size), half),
            pltpu.VMEM((size, seqs * (rows + text_rows)), half),
            pltpu.VMEM((rows + text_rows, size), jnp.float32),
            pltpu.VMEM((seqs, sections, rows // sections, size), half),
            pltpu.VMEM((seqs, text_rows, size), half),
            pltpu.VMEM((rows + text_rows, width), half),
            pltpu.VMEM((rows + text_rows, width), half),
            pltpu.VMEM((rows + text_rows, width), half),
            dma((4, heads)),
            dma((4, seqs)),
            dma((seqs, sections)),
            dma((seqs,)),
            dma((sections * heads,)),
            dma((heads,)),
            pltpu.SemaphoreType.REGULAR,
            dma((6,)),
        ],
        compiler_params=pltpu.CompilerParams(
            collective_id=0, has_side_effects=True, vmem_limit_bytes=60 * 1024 * 1024
        ),
    )(q_img, k_img, v_img, q_txt, k_txt, v_txt, norm_gains, block_map)
    return (image_flat.reshape(rows // sections, 1, sections * width), text_out)


def one_head_fits(rows, text_rows, heads, head_size, key_blocks, seqs, sections):
    return (
        rows == BLOCK
        and head_size == BLOCK
        and seqs == heads + 2
        and seqs & (seqs - 1) == 0
        and key_blocks == seqs
        and seqs % 8 == 0
        and text_rows % 16 == 0
        and (seqs * text_rows) % (2 * BLOCK) == 0
        and rows % (16 * sections) == 0
        and sections % 2 == 0
    )


def layer(q_img, k_img, v_img, q_txt, k_txt, v_txt, norm_gains, block_map):
    rows, width = q_img.shape
    head_size = norm_gains.shape[1]
    fits = one_head_fits(
        rows,
        q_txt.shape[0],
        width // head_size,
        head_size,
        block_map.shape[2],
        lax.axis_size("seq"),
        lax.axis_size("section"),
    )
    chosen = by_heads if fits else body
    return chosen(q_img, k_img, v_img, q_txt, k_txt, v_txt, norm_gains, block_map)


def solution(mesh):
    placed = (
        P("seq", "section"),
        P("seq", "section"),
        P("seq", "section"),
        P("seq", "section"),
        P("seq", "section"),
        P("seq", "section"),
        P(),
        P("section", "seq", None),
    )
    return jax.shard_map(
        layer,
        mesh=mesh,
        in_specs=placed,
        out_specs=(P("seq", "section", None), P("seq", "section")),
        check_vma=False,
    )
```

```python
import functools
import math

import jax
import jax.numpy as jnp
from jax import lax
from jax.experimental import pallas as pl
from jax.experimental.pallas import tpu as pltpu
from jax.sharding import PartitionSpec as P

BLOCK = 128


def normed(values, gain, heads):
    rows = values.shape[0]
    floats = values.astype(jnp.float32).reshape(rows, heads, gain.shape[0])
    power = jnp.mean(floats * floats, axis=-1, keepdims=True)
    return (floats * lax.rsqrt(power + 1e-06) * gain).astype(jnp.bfloat16)


def make_keep(flags, query_shards, shards, first, rows, text_rows):
    heads = flags.shape[0]
    key_blocks = rows // BLOCK
    stride = rows + text_rows
    picked = lax.dynamic_slice_in_dim(flags, first * key_blocks, shards * key_blocks, 2)
    picked = picked.reshape(heads, query_shards, key_blocks, shards, key_blocks)
    image_mask = jnp.broadcast_to(
        picked[:, :, :, None, :, :, None] > 0,
        (heads, query_shards, key_blocks, BLOCK, shards, key_blocks, BLOCK),
    )
    image_mask = image_mask.reshape(heads, query_shards, rows, shards, rows)
    keep = jnp.pad(
        image_mask, ((0, 0), (0, 0), (0, text_rows), (0, 0), (0, text_rows)), constant_values=True
    )
    return keep.reshape(heads, query_shards * stride, shards, stride)


def accumulate(queries, flags, query_shards, rows, text_rows, carry, pieces, start):
    numer, denom = carry
    piece_keys, piece_values = pieces
    heads = queries.shape[1]
    head_size = queries.shape[2]
    stride = rows + text_rows
    shards = piece_keys.shape[0] // stride
    first = start // stride
    keys_four = piece_keys.reshape(shards, stride, heads, head_size)
    values_four = piece_values.reshape(shards, stride, heads, head_size)
    scores = jnp.einsum(
        "qhd,skhd->hqsk", queries, keys_four, preferred_element_type=jnp.float32
    ) * head_size ** (-0.5)
    keep = make_keep(flags, query_shards, shards, first, rows, text_rows)
    weights = jnp.where(keep, jnp.exp(scores), jnp.float32(0.0))
    denom = denom + jnp.sum(weights, axis=(2, 3))
    numer = numer + jnp.einsum(
        "hqsk,skhd->hqd",
        weights.astype(jnp.bfloat16),
        values_four,
        preferred_element_type=jnp.float32,
    )
    return (numer, denom)


def body(q_img, k_img, v_img, q_txt, k_txt, v_txt, norm_gains, block_map):
    rows, width = q_img.shape
    head_size = norm_gains.shape[1]
    heads = width // head_size
    text_rows = q_txt.shape[0]
    stride = rows + text_rows
    queries = jnp.concatenate(
        [normed(q_img, norm_gains[0], heads), normed(q_txt, norm_gains[2], heads)], axis=0
    )
    keys_image = normed(k_img, norm_gains[1], heads).reshape(rows, width)
    keys_text = normed(k_txt, norm_gains[3], heads).reshape(text_rows, width)
    local_keys = jnp.concatenate([keys_image, keys_text], axis=0)
    local_values = jnp.concatenate([v_img, v_txt], axis=0)
    start_state = (
        jnp.zeros((heads, stride, head_size), jnp.float32),
        jnp.zeros((heads, stride), jnp.float32),
    )

    def fold_step(carry, pieces, start):
        return accumulate(queries, block_map, 1, rows, text_rows, carry, pieces, start)

    whole_keys, whole_values = (
        lax.all_gather(local_keys, "seq", axis=0, tiled=True),
        lax.all_gather(local_values, "seq", axis=0, tiled=True),
    )
    count_seq = lax.axis_size("seq")
    grouped = 1
    while (
        grouped * 2 <= count_seq
        and count_seq % (grouped * 2) == 0
        and (grouped * 2 * stride <= 1024)
    ):
        grouped = grouped * 2
    span = grouped * stride

    def step_over(index, carry):
        offset = index * span
        piece_keys = lax.dynamic_slice_in_dim(whole_keys, offset, span, 0)
        piece_values = lax.dynamic_slice_in_dim(whole_values, offset, span, 0)
        return fold_step(carry, (piece_keys, piece_values), offset)

    numer, denom = lax.fori_loop(0, count_seq // grouped, step_over, start_state)
    result = numer / denom[..., None]
    merged = result.transpose(1, 0, 2).reshape(stride, width).astype(jnp.bfloat16)
    image_part = merged[:rows]
    text_out = merged[rows:]
    sections = lax.axis_size("section")
    image_out = lax.all_to_all(
        image_part.reshape(rows // sections, sections, width),
        "section",
        split_axis=1,
        concat_axis=2,
        tiled=True,
    )
    return (image_out, text_out)


def owner_of(head):
    return head + 1


def partner(place, step, count):
    total = 0
    bit = 1
    while bit < count:
        total = total + bit * lax.rem(lax.div(place, bit) + lax.div(step, bit), 2)
        bit *= 2
    return total


def head_kernel(
    heads, seqs, sections,
    q_img, k_img, v_img, q_txt, k_txt, v_txt, gains, flags_in,
    image_out, text_out,
    flags_own, flags_got, q_got, k_got, v_got, values, keys_t, total,
    image_stage, text_stage,
    held_q, held_k, held_v,
    send_sem, recv_sem, image_sent, text_sent, image_recv, text_recv, ready, load_sem,
):
    rows = q_img.shape[0]
    text_rows = q_txt.shape[0]
    size = gains.shape[1]
    key_blocks = flags_in.shape[2]
    part = rows // sections
    all_rows = seqs * rows
    factor = size ** (-0.5) * math.log2(math.e)
    section = lax.axis_index("section")
    me = lax.axis_index("seq")

    near = heads // 2

    barrier = pltpu.get_barrier_semaphore()

    loads = [
        pltpu.make_async_copy(source, target, load_sem.at[index])
        for index, (source, target) in enumerate(
            (
                (k_img, held_k.at[:rows]),
                (k_txt, held_k.at[rows:]),
                (v_img, held_v.at[:rows]),
                (v_txt, held_v.at[rows:]),
                (q_img, held_q.at[:rows]),
                (q_txt, held_q.at[rows:]),
            )
        )
    ]

    def signal(semaphore, **place):
        pl.semaphore_signal(
            semaphore, inc=1, device_id=place, device_id_type=pl.DeviceIdType.MESH
        )

    for step in range(1, seqs):
        signal(barrier, seq=lax.rem(me + step, seqs))
    for step in range(1, sections):
        signal(barrier, section=lax.rem(section + step, sections))
    for load in loads:
        load.start()
    for head in range(heads):
        for block in range(key_blocks):
            flags_own[head, block : block + 1, :] = jnp.full(
                (1, flags_own.shape[2]), flags_in[head, 0, block], jnp.int32
            )
    pl.semaphore_wait(barrier, sections + seqs - 2)
    for step in range(1, sections):
        signal(ready, section=lax.rem(section + step, sections))

    def landing(kind, source):
        if kind == 0:
            return flags_got.at[source]
        return (k_got, v_got, q_got)[kind - 1].at[source]

    operands = (None, held_k, held_v, held_q)

    def leaving(kind, head):
        if kind == 0:
            return flags_own.at[head]
        return operands[kind].at[:, pl.ds(pl.multiple_of(head * size, size), size)]

    def outward(kind, head):
        return pltpu.make_async_remote_copy(
            src_ref=leaving(kind, head),
            dst_ref=landing(kind, me),
            send_sem=send_sem.at[kind, head],
            recv_sem=recv_sem.at[kind, me],
            device_id={"seq": owner_of(head)},
            device_id_type=pl.DeviceIdType.MESH,
        )

    def inward(kind, source):
        place = landing(kind, source)
        return pltpu.make_async_copy(place, place, recv_sem.at[kind, source])

    for group in ((0, 1), (2,), (3,)):
        for kind in group:
            if kind > 0:
                loads[2 * kind - 2].wait()
                loads[2 * kind - 1].wait()

        def send_group(step, carry):
            turn = lax.rem(lax.div(step, near) + 1 - lax.div(me, seqs // 2), 2)
            head = turn * near + lax.rem(step + me, near)
            target = owner_of(head)

            @pl.when(target != me)
            def _():
                for kind in group:
                    outward(kind, head).start()

            @pl.when(target == me)
            def _():
                for kind in group:
                    pltpu.make_async_copy(
                        leaving(kind, head), landing(kind, me), recv_sem.at[kind, me]
                    ).start()

            return carry

        lax.fori_loop(0, heads, send_group, 0)

    def scaled(block, gain_row):
        floats = block.astype(jnp.float32)
        power = jnp.mean(floats * floats, axis=-1, keepdims=True)
        return floats * lax.rsqrt(power + 1e-06) * gains[gain_row : gain_row + 1, :]

    my_head = me - 1
    mine = jnp.logical_and(my_head >= 0, my_head < heads)

    def image_copy(chunk, to_section):
        column = pl.multiple_of((section * heads + my_head) * size, size)
        return (
            image_stage.at[chunk, to_section],
            image_out.at[:, pl.ds(column, size)],
        )

    def image_remote(chunk, to_section):
        source, target = image_copy(chunk, to_section)
        return pltpu.make_async_remote_copy(
            src_ref=source,
            dst_ref=target,
            send_sem=image_sent.at[chunk, to_section],
            recv_sem=image_recv.at[section * heads + my_head],
            device_id={"section": to_section, "seq": chunk},
            device_id_type=pl.DeviceIdType.MESH,
        )

    def text_copy(chunk):
        return (
            text_stage.at[chunk],
            text_out.at[:, pl.ds(pl.multiple_of(my_head * size, size), size)],
        )

    def text_remote(chunk):
        source, target = text_copy(chunk)
        return pltpu.make_async_remote_copy(
            src_ref=source,
            dst_ref=target,
            send_sem=text_sent.at[chunk],
            recv_sem=text_recv.at[my_head],
            device_id={"seq": chunk},
            device_id_type=pl.DeviceIdType.MESH,
        )

    pl.semaphore_wait(ready, sections - 1)

    @pl.when(mine)
    def _():
        def take_keys(step, carry):
            source = partner(me, step, seqs)
            inward(0, source).wait()
            inward(1, source).wait()
            keys_t[:, pl.ds(pl.multiple_of(source * rows, rows), rows)] = (
                scaled(k_got[source, :rows], 1).T.astype(jnp.bfloat16)
            )
            return carry

        lax.fori_loop(0, seqs, take_keys, 0)
        text_keys = k_got[:, rows:].reshape(seqs * text_rows, size)
        keys_t[:, all_rows:] = scaled(text_keys, 3).T.astype(jnp.bfloat16)

        def take_values(step, carry):
            source = partner(me, step, seqs)
            inward(2, source).wait()
            image_place = pl.ds(pl.multiple_of(source * rows, rows), rows)
            values[image_place, :] = v_got[source, :rows]
            text_place = pl.multiple_of(all_rows + source * text_rows, text_rows)
            values[pl.ds(text_place, text_rows), :] = v_got[source, rows:]
            return carry

        lax.fori_loop(0, seqs, take_values, 0)

        def answer(step, carry):
            chunk = partner(me, lax.rem(step + seqs // 2, seqs), seqs)
            inward(3, chunk).wait()
            queries = jnp.concatenate(
                [scaled(q_got[chunk, :rows], 0), scaled(q_got[chunk, rows:], 2)], axis=0
            ).astype(jnp.bfloat16)
            flags = flags_got[chunk]
            numer = jnp.zeros((rows + text_rows, size), jnp.float32)
            denom = jnp.zeros((rows + text_rows, rows), jnp.float32)
            width = 2 * rows
            for first in range(0, keys_t.shape[1], width):
                scores = jnp.dot(
                    queries, keys_t[:, first : first + width], preferred_element_type=jnp.float32
                )
                weights = jnp.exp2(scores * factor)
                halves = []
                for half in range(2):
                    piece = weights[:, half * rows : (half + 1) * rows]
                    block = first // rows + half
                    if first < all_rows:
                        kept = jnp.where(flags[block : block + 1, :] > 0, piece[:rows], 0.0)
                        piece = jnp.concatenate([kept, piece[rows:]], axis=0)
                    denom = denom + piece
                    halves.append(piece.astype(jnp.bfloat16))
                numer = numer + jnp.dot(
                    jnp.concatenate(halves, axis=1),
                    values[first : first + width, :],
                    preferred_element_type=jnp.float32,
                )
            total[...] = numer / jnp.sum(denom, axis=-1, keepdims=True)
            for to_section in range(sections):
                image_stage[chunk, to_section] = total[
                    pl.ds(to_section, part, stride=sections), :
                ].astype(jnp.bfloat16)
            text_stage[chunk] = total[rows:, :].astype(jnp.bfloat16)
            for to_section in range(sections):
                here = jnp.logical_and(section == to_section, chunk == me)

                @pl.when(jnp.logical_not(here))
                def _():
                    image_remote(chunk, to_section).start()

                @pl.when(here)
                def _():
                    source, target = image_copy(chunk, to_section)
                    pltpu.make_async_copy(
                        source, target, image_recv.at[section * heads + my_head]
                    ).start()

            @pl.when(chunk != me)
            def _():
                text_remote(chunk).start()

            @pl.when(chunk == me)
            def _():
                source, target = text_copy(chunk)
                pltpu.make_async_copy(source, target, text_recv.at[my_head]).start()

            return carry

        lax.fori_loop(0, seqs, answer, 0)

    def finish_group(step, carry):
        head = lax.rem(step + me, heads)

        @pl.when(owner_of(head) != me)
        def _():
            for kind in range(4):
                outward(kind, head).wait_send()

        return carry

    lax.fori_loop(0, heads, finish_group, 0)

    @pl.when(mine)
    def _():
        def sent(chunk, carry):
            for to_section in range(sections):

                @pl.when(jnp.logical_or(section != to_section, chunk != me))
                def _():
                    image_remote(chunk, to_section).wait_send()

            @pl.when(chunk != me)
            def _():
                text_remote(chunk).wait_send()

            return carry

        lax.fori_loop(0, seqs, sent, 0)

    def arrived(head, carry):
        place = image_out.at[:, pl.ds(pl.multiple_of(head * size, size), size)]
        pltpu.make_async_copy(place, place, image_recv.at[head]).wait()
        return carry

    lax.fori_loop(0, sections * heads, arrived, 0)

    def text_arrived(head, carry):
        place = text_out.at[:, pl.ds(pl.multiple_of(head * size, size), size)]
        pltpu.make_async_copy(place, place, text_recv.at[head]).wait()
        return carry

    lax.fori_loop(0, heads, text_arrived, 0)


def by_heads(q_img, k_img, v_img, q_txt, k_txt, v_txt, norm_gains, block_map):
    rows, width = q_img.shape
    size = norm_gains.shape[1]
    heads = width // size
    text_rows = q_txt.shape[0]
    seqs = lax.axis_size("seq")
    sections = lax.axis_size("section")
    half = jnp.bfloat16
    flags_shape = (block_map.shape[2], size)
    anywhere = pl.BlockSpec(memory_space=pl.ANY)
    dma = pltpu.SemaphoreType.DMA
    image_flat, text_out = pl.pallas_call(
        functools.partial(head_kernel, heads, seqs, sections),
        out_shape=(
            jax.ShapeDtypeStruct((rows // sections, sections * width), half),
            jax.ShapeDtypeStruct((text_rows, width), half),
        ),
        in_specs=[anywhere] * 6
        + [pl.BlockSpec(memory_space=pltpu.VMEM), pl.BlockSpec(memory_space=pltpu.SMEM)],
        out_specs=(anywhere, anywhere),
        scratch_shapes=[
            pltpu.VMEM((heads,) + flags_shape, jnp.int32),
            pltpu.VMEM((seqs,) + flags_shape, jnp.int32),
            pltpu.VMEM((seqs, rows + text_rows, size), half),
            pltpu.VMEM((seqs, rows + text_rows, size), half),
            pltpu.VMEM((seqs, rows + text_rows, size), half),
            pltpu.VMEM((seqs * (rows + text_rows), size), half),
            pltpu.VMEM((size, seqs * (rows + text_rows)), half),
            pltpu.VMEM((rows + text_rows, size), jnp.float32),
            pltpu.VMEM((seqs, sections, rows // sections, size), half),
            pltpu.VMEM((seqs, text_rows, size), half),
            pltpu.VMEM((rows + text_rows, width), half),
            pltpu.VMEM((rows + text_rows, width), half),
            pltpu.VMEM((rows + text_rows, width), half),
            dma((4, heads)),
            dma((4, seqs)),
            dma((seqs, sections)),
            dma((seqs,)),
            dma((sections * heads,)),
            dma((heads,)),
            pltpu.SemaphoreType.REGULAR,
            dma((6,)),
        ],
        compiler_params=pltpu.CompilerParams(
            collective_id=0, has_side_effects=True, vmem_limit_bytes=60 * 1024 * 1024
        ),
    )(q_img, k_img, v_img, q_txt, k_txt, v_txt, norm_gains, block_map)
    return (image_flat.reshape(rows // sections, 1, sections * width), text_out)


def one_head_fits(rows, text_rows, heads, head_size, key_blocks, seqs, sections):
    return (
        rows == BLOCK
        and head_size == BLOCK
        and seqs == heads + 2
        and seqs & (seqs - 1) == 0
        and key_blocks == seqs
        and seqs % 8 == 0
        and text_rows % 16 == 0
        and (seqs * text_rows) % (2 * BLOCK) == 0
        and rows % (16 * sections) == 0
        and sections % 2 == 0
    )


def layer(q_img, k_img, v_img, q_txt, k_txt, v_txt, norm_gains, block_map):
    rows, width = q_img.shape
    head_size = norm_gains.shape[1]
    fits = one_head_fits(
        rows,
        q_txt.shape[0],
        width // head_size,
        head_size,
        block_map.shape[2],
        lax.axis_size("seq"),
        lax.axis_size("section"),
    )
    chosen = by_heads if fits else body
    return chosen(q_img, k_img, v_img, q_txt, k_txt, v_txt, norm_gains, block_map)


def solution(mesh):
    placed = (
        P("seq", "section"),
        P("seq", "section"),
        P("seq", "section"),
        P("seq", "section"),
        P("seq", "section"),
        P("seq", "section"),
        P(),
        P("section", "seq", None),
    )
    return jax.shard_map(
        layer,
        mesh=mesh,
        in_specs=placed,
        out_specs=(P("seq", "section", None), P("seq", "section")),
        check_vma=False,
    )
```

```python
import functools
import math

import jax
import jax.numpy as jnp
from jax import lax
from jax.experimental import pallas as pl
from jax.experimental.pallas import tpu as pltpu
from jax.sharding import PartitionSpec as P

BLOCK = 128


def normed(values, gain, heads):
    rows = values.shape[0]
    floats = values.astype(jnp.float32).reshape(rows, heads, gain.shape[0])
    power = jnp.mean(floats * floats, axis=-1, keepdims=True)
    return (floats * lax.rsqrt(power + 1e-06) * gain).astype(jnp.bfloat16)


def make_keep(flags, query_shards, shards, first, rows, text_rows):
    heads = flags.shape[0]
    key_blocks = rows // BLOCK
    stride = rows + text_rows
    picked = lax.dynamic_slice_in_dim(flags, first * key_blocks, shards * key_blocks, 2)
    picked = picked.reshape(heads, query_shards, key_blocks, shards, key_blocks)
    image_mask = jnp.broadcast_to(
        picked[:, :, :, None, :, :, None] > 0,
        (heads, query_shards, key_blocks, BLOCK, shards, key_blocks, BLOCK),
    )
    image_mask = image_mask.reshape(heads, query_shards, rows, shards, rows)
    keep = jnp.pad(
        image_mask, ((0, 0), (0, 0), (0, text_rows), (0, 0), (0, text_rows)), constant_values=True
    )
    return keep.reshape(heads, query_shards * stride, shards, stride)


def accumulate(queries, flags, query_shards, rows, text_rows, carry, pieces, start):
    numer, denom = carry
    piece_keys, piece_values = pieces
    heads = queries.shape[1]
    head_size = queries.shape[2]
    stride = rows + text_rows
    shards = piece_keys.shape[0] // stride
    first = start // stride
    keys_four = piece_keys.reshape(shards, stride, heads, head_size)
    values_four = piece_values.reshape(shards, stride, heads, head_size)
    scores = jnp.einsum(
        "qhd,skhd->hqsk", queries, keys_four, preferred_element_type=jnp.float32
    ) * head_size ** (-0.5)
    keep = make_keep(flags, query_shards, shards, first, rows, text_rows)
    weights = jnp.where(keep, jnp.exp(scores), jnp.float32(0.0))
    denom = denom + jnp.sum(weights, axis=(2, 3))
    numer = numer + jnp.einsum(
        "hqsk,skhd->hqd",
        weights.astype(jnp.bfloat16),
        values_four,
        preferred_element_type=jnp.float32,
    )
    return (numer, denom)


def body(q_img, k_img, v_img, q_txt, k_txt, v_txt, norm_gains, block_map):
    rows, width = q_img.shape
    head_size = norm_gains.shape[1]
    heads = width // head_size
    text_rows = q_txt.shape[0]
    stride = rows + text_rows
    queries = jnp.concatenate(
        [normed(q_img, norm_gains[0], heads), normed(q_txt, norm_gains[2], heads)], axis=0
    )
    keys_image = normed(k_img, norm_gains[1], heads).reshape(rows, width)
    keys_text = normed(k_txt, norm_gains[3], heads).reshape(text_rows, width)
    local_keys = jnp.concatenate([keys_image, keys_text], axis=0)
    local_values = jnp.concatenate([v_img, v_txt], axis=0)
    start_state = (
        jnp.zeros((heads, stride, head_size), jnp.float32),
        jnp.zeros((heads, stride), jnp.float32),
    )

    def fold_step(carry, pieces, start):
        return accumulate(queries, block_map, 1, rows, text_rows, carry, pieces, start)

    whole_keys, whole_values = (
        lax.all_gather(local_keys, "seq", axis=0, tiled=True),
        lax.all_gather(local_values, "seq", axis=0, tiled=True),
    )
    count_seq = lax.axis_size("seq")
    grouped = 1
    while (
        grouped * 2 <= count_seq
        and count_seq % (grouped * 2) == 0
        and (grouped * 2 * stride <= 1024)
    ):
        grouped = grouped * 2
    span = grouped * stride

    def step_over(index, carry):
        offset = index * span
        piece_keys = lax.dynamic_slice_in_dim(whole_keys, offset, span, 0)
        piece_values = lax.dynamic_slice_in_dim(whole_values, offset, span, 0)
        return fold_step(carry, (piece_keys, piece_values), offset)

    numer, denom = lax.fori_loop(0, count_seq // grouped, step_over, start_state)
    result = numer / denom[..., None]
    merged = result.transpose(1, 0, 2).reshape(stride, width).astype(jnp.bfloat16)
    image_part = merged[:rows]
    text_out = merged[rows:]
    sections = lax.axis_size("section")
    image_out = lax.all_to_all(
        image_part.reshape(rows // sections, sections, width),
        "section",
        split_axis=1,
        concat_axis=2,
        tiled=True,
    )
    return (image_out, text_out)


def owner_of(head):
    return head + 1


def partner(place, step, count):
    total = 0
    bit = 1
    while bit < count:
        total = total + bit * lax.rem(lax.div(place, bit) + lax.div(step, bit), 2)
        bit *= 2
    return total


def head_kernel(
    heads, seqs, sections,
    q_img, k_img, v_img, q_txt, k_txt, v_txt, gains, flags_in,
    image_out, text_out,
    flags_own, flags_got, q_got, k_got, v_got, values, keys_t, total,
    image_stage, text_stage,
    held_q, held_k, held_v,
    send_sem, recv_sem, image_sent, text_sent, image_recv, text_recv, ready, load_sem,
):
    rows = q_img.shape[0]
    text_rows = q_txt.shape[0]
    size = gains.shape[1]
    key_blocks = flags_in.shape[2]
    part = rows // sections
    all_rows = seqs * rows
    factor = size ** (-0.5) * math.log2(math.e)
    section = lax.axis_index("section")
    me = lax.axis_index("seq")

    near = heads // 2

    barrier = pltpu.get_barrier_semaphore()

    loads = [
        pltpu.make_async_copy(source, target, load_sem.at[index])
        for index, (source, target) in enumerate(
            (
                (k_img, held_k.at[:rows]),
                (k_txt, held_k.at[rows:]),
                (v_img, held_v.at[:rows]),
                (v_txt, held_v.at[rows:]),
                (q_img, held_q.at[:rows]),
                (q_txt, held_q.at[rows:]),
            )
        )
    ]

    def signal(semaphore, **place):
        pl.semaphore_signal(
            semaphore, inc=1, device_id=place, device_id_type=pl.DeviceIdType.MESH
        )

    for step in range(1, seqs):
        signal(barrier, seq=lax.rem(me + step, seqs))
    for step in range(1, sections):
        signal(barrier, section=lax.rem(section + step, sections))
    for load in loads:
        load.start()
    for head in range(heads):
        for block in range(key_blocks):
            flags_own[head, block : block + 1, :] = jnp.full(
                (1, flags_own.shape[2]), flags_in[head, 0, block], jnp.int32
            )
    pl.semaphore_wait(barrier, sections + seqs - 2)
    for step in range(1, sections):
        signal(ready, section=lax.rem(section + step, sections))

    def landing(kind, source):
        if kind == 0:
            return flags_got.at[source]
        return (k_got, v_got, q_got)[kind - 1].at[source]

    operands = (None, held_k, held_v, held_q)

    def leaving(kind, head):
        if kind == 0:
            return flags_own.at[head]
        return operands[kind].at[:, pl.ds(pl.multiple_of(head * size, size), size)]

    def outward(kind, head):
        return pltpu.make_async_remote_copy(
            src_ref=leaving(kind, head),
            dst_ref=landing(kind, me),
            send_sem=send_sem.at[kind, head],
            recv_sem=recv_sem.at[kind, me],
            device_id={"seq": owner_of(head)},
            device_id_type=pl.DeviceIdType.MESH,
        )

    def inward(kind, source):
        place = landing(kind, source)
        return pltpu.make_async_copy(place, place, recv_sem.at[kind, source])

    for group in ((0, 1), (2,), (3,)):
        for kind in group:
            if kind > 0:
                loads[2 * kind - 2].wait()
                loads[2 * kind - 1].wait()

        def send_group(step, carry):
            turn = lax.rem(lax.div(step, near) + 1 - lax.div(me, seqs // 2), 2)
            head = turn * near + lax.rem(step + me, near)
            target = owner_of(head)

            @pl.when(target != me)
            def _():
                for kind in group:
                    outward(kind, head).start()

            @pl.when(target == me)
            def _():
                for kind in group:
                    pltpu.make_async_copy(
                        leaving(kind, head), landing(kind, me), recv_sem.at[kind, me]
                    ).start()

            return carry

        lax.fori_loop(0, heads, send_group, 0)

    def scaled(block, gain_row):
        floats = block.astype(jnp.float32)
        power = jnp.mean(floats * floats, axis=-1, keepdims=True)
        return floats * lax.rsqrt(power + 1e-06) * gains[gain_row : gain_row + 1, :]

    my_head = me - 1
    mine = jnp.logical_and(my_head >= 0, my_head < heads)

    def image_copy(chunk, to_section):
        column = pl.multiple_of((section * heads + my_head) * size, size)
        return (
            image_stage.at[chunk, to_section],
            image_out.at[:, pl.ds(column, size)],
        )

    def image_remote(chunk, to_section):
        source, target = image_copy(chunk, to_section)
        return pltpu.make_async_remote_copy(
            src_ref=source,
            dst_ref=target,
            send_sem=image_sent.at[chunk, to_section],
            recv_sem=image_recv.at[0],
            device_id={"section": to_section, "seq": chunk},
            device_id_type=pl.DeviceIdType.MESH,
        )

    def text_copy(chunk):
        return (
            text_stage.at[chunk],
            text_out.at[:, pl.ds(pl.multiple_of(my_head * size, size), size)],
        )

    def text_remote(chunk):
        source, target = text_copy(chunk)
        return pltpu.make_async_remote_copy(
            src_ref=source,
            dst_ref=target,
            send_sem=text_sent.at[chunk],
            recv_sem=text_recv.at[0],
            device_id={"seq": chunk},
            device_id_type=pl.DeviceIdType.MESH,
        )

    pl.semaphore_wait(ready, sections - 1)

    @pl.when(mine)
    def _():
        def take_keys(step, carry):
            source = partner(me, step, seqs)
            inward(0, source).wait()
            inward(1, source).wait()
            keys_t[:, pl.ds(pl.multiple_of(source * rows, rows), rows)] = (
                scaled(k_got[source, :rows], 1).T.astype(jnp.bfloat16)
            )
            return carry

        lax.fori_loop(0, seqs, take_keys, 0)
        text_keys = k_got[:, rows:].reshape(seqs * text_rows, size)
        keys_t[:, all_rows:] = scaled(text_keys, 3).T.astype(jnp.bfloat16)

        def take_values(step, carry):
            source = partner(me, step, seqs)
            inward(2, source).wait()
            image_place = pl.ds(pl.multiple_of(source * rows, rows), rows)
            values[image_place, :] = v_got[source, :rows]
            text_place = pl.multiple_of(all_rows + source * text_rows, text_rows)
            values[pl.ds(text_place, text_rows), :] = v_got[source, rows:]
            return carry

        lax.fori_loop(0, seqs, take_values, 0)

        def answer(step, carry):
            chunk = partner(me, lax.rem(step + seqs // 2, seqs), seqs)
            inward(3, chunk).wait()
            queries = jnp.concatenate(
                [scaled(q_got[chunk, :rows], 0), scaled(q_got[chunk, rows:], 2)], axis=0
            ).astype(jnp.bfloat16)
            flags = flags_got[chunk]
            numer = jnp.zeros((rows + text_rows, size), jnp.float32)
            denom = jnp.zeros((rows + text_rows, rows), jnp.float32)
            width = 2 * rows
            for first in range(0, keys_t.shape[1], width):
                scores = jnp.dot(
                    queries, keys_t[:, first : first + width], preferred_element_type=jnp.float32
                )
                weights = jnp.exp2(scores * factor)
                halves = []
                for half in range(2):
                    piece = weights[:, half * rows : (half + 1) * rows]
                    block = first // rows + half
                    if first < all_rows:
                        kept = jnp.where(flags[block : block + 1, :] > 0, piece[:rows], 0.0)
                        piece = jnp.concatenate([kept, piece[rows:]], axis=0)
                    denom = denom + piece
                    halves.append(piece.astype(jnp.bfloat16))
                numer = numer + jnp.dot(
                    jnp.concatenate(halves, axis=1),
                    values[first : first + width, :],
                    preferred_element_type=jnp.float32,
                )
            total[...] = numer / jnp.sum(denom, axis=-1, keepdims=True)
            for to_section in range(sections):
                image_stage[chunk, to_section] = total[
                    pl.ds(to_section, part, stride=sections), :
                ].astype(jnp.bfloat16)
            text_stage[chunk] = total[rows:, :].astype(jnp.bfloat16)
            for to_section in range(sections):
                here = jnp.logical_and(section == to_section, chunk == me)

                @pl.when(jnp.logical_not(here))
                def _():
                    image_remote(chunk, to_section).start()

                @pl.when(here)
                def _():
                    source, target = image_copy(chunk, to_section)
                    pltpu.make_async_copy(
                        source, target, image_recv.at[0]
                    ).start()

            @pl.when(chunk != me)
            def _():
                text_remote(chunk).start()

            @pl.when(chunk == me)
            def _():
                source, target = text_copy(chunk)
                pltpu.make_async_copy(source, target, text_recv.at[0]).start()

            return carry

        lax.fori_loop(0, seqs, answer, 0)

    def finish_group(step, carry):
        head = lax.rem(step + me, heads)

        @pl.when(owner_of(head) != me)
        def _():
            for kind in range(4):
                outward(kind, head).wait_send()

        return carry

    lax.fori_loop(0, heads, finish_group, 0)

    @pl.when(mine)
    def _():
        def sent(chunk, carry):
            for to_section in range(sections):

                @pl.when(jnp.logical_or(section != to_section, chunk != me))
                def _():
                    image_remote(chunk, to_section).wait_send()

            @pl.when(chunk != me)
            def _():
                text_remote(chunk).wait_send()

            return carry

        lax.fori_loop(0, seqs, sent, 0)

    pltpu.make_async_copy(image_out, image_out, image_recv.at[0]).wait()
    pltpu.make_async_copy(text_out, text_out, text_recv.at[0]).wait()


def by_heads(q_img, k_img, v_img, q_txt, k_txt, v_txt, norm_gains, block_map):
    rows, width = q_img.shape
    size = norm_gains.shape[1]
    heads = width // size
    text_rows = q_txt.shape[0]
    seqs = lax.axis_size("seq")
    sections = lax.axis_size("section")
    half = jnp.bfloat16
    flags_shape = (block_map.shape[2], size)
    anywhere = pl.BlockSpec(memory_space=pl.ANY)
    dma = pltpu.SemaphoreType.DMA
    image_flat, text_out = pl.pallas_call(
        functools.partial(head_kernel, heads, seqs, sections),
        out_shape=(
            jax.ShapeDtypeStruct((rows // sections, sections * width), half),
            jax.ShapeDtypeStruct((text_rows, width), half),
        ),
        in_specs=[anywhere] * 6
        + [pl.BlockSpec(memory_space=pltpu.VMEM), pl.BlockSpec(memory_space=pltpu.SMEM)],
        out_specs=(anywhere, anywhere),
        scratch_shapes=[
            pltpu.VMEM((heads,) + flags_shape, jnp.int32),
            pltpu.VMEM((seqs,) + flags_shape, jnp.int32),
            pltpu.VMEM((seqs, rows + text_rows, size), half),
            pltpu.VMEM((seqs, rows + text_rows, size), half),
            pltpu.VMEM((seqs, rows + text_rows, size), half),
            pltpu.VMEM((seqs * (rows + text_rows), size), half),
            pltpu.VMEM((size, seqs * (rows + text_rows)), half),
            pltpu.VMEM((rows + text_rows, size), jnp.float32),
            pltpu.VMEM((seqs, sections, rows // sections, size), half),
            pltpu.VMEM((seqs, text_rows, size), half),
            pltpu.VMEM((rows + text_rows, width), half),
            pltpu.VMEM((rows + text_rows, width), half),
            pltpu.VMEM((rows + text_rows, width), half),
            dma((4, heads)),
            dma((4, seqs)),
            dma((seqs, sections)),
            dma((seqs,)),
            dma((1,)),
            dma((1,)),
            pltpu.SemaphoreType.REGULAR,
            dma((6,)),
        ],
        compiler_params=pltpu.CompilerParams(
            collective_id=0, has_side_effects=True, vmem_limit_bytes=60 * 1024 * 1024
        ),
    )(q_img, k_img, v_img, q_txt, k_txt, v_txt, norm_gains, block_map)
    return (image_flat.reshape(rows // sections, 1, sections * width), text_out)


def one_head_fits(rows, text_rows, heads, head_size, key_blocks, seqs, sections):
    return (
        rows == BLOCK
        and head_size == BLOCK
        and seqs == heads + 2
        and seqs & (seqs - 1) == 0
        and key_blocks == seqs
        and seqs % 8 == 0
        and text_rows % 16 == 0
        and (seqs * text_rows) % (2 * BLOCK) == 0
        and rows % (16 * sections) == 0
        and sections % 2 == 0
    )


def layer(q_img, k_img, v_img, q_txt, k_txt, v_txt, norm_gains, block_map):
    rows, width = q_img.shape
    head_size = norm_gains.shape[1]
    fits = one_head_fits(
        rows,
        q_txt.shape[0],
        width // head_size,
        head_size,
        block_map.shape[2],
        lax.axis_size("seq"),
        lax.axis_size("section"),
    )
    chosen = by_heads if fits else body
    return chosen(q_img, k_img, v_img, q_txt, k_txt, v_txt, norm_gains, block_map)


def solution(mesh):
    placed = (
        P("seq", "section"),
        P("seq", "section"),
        P("seq", "section"),
        P("seq", "section"),
        P("seq", "section"),
        P("seq", "section"),
        P(),
        P("section", "seq", None),
    )
    return jax.shard_map(
        layer,
        mesh=mesh,
        in_specs=placed,
        out_specs=(P("seq", "section", None), P("seq", "section")),
        check_vma=False,
    )
```
